32 devices in a mesh: tm: 4 (over x, core), tmpl: 8 (over z, y).
Axes of the slice: x: 2, y: 2, z: 4, core: 2. Of those that a mesh axis runs over, the one named last changes fastest.
Arguments:
- strain: float32 [2, 786432], P(None, 'tm'), may hold values from -24 to 24
- segment_valid: int32 [2, 3072], P(None, 'tm'), may hold values 0 or 1
- templates: float32 [16, 512], P('tmpl'), may hold values from -6 to 6
- durations: int32 [16], P('tmpl'), may hold values from 128 to 512
- bin_edges: int32 [16, 15], P('tmpl'), may hold values from 1 to 255, as said below
Outputs:
- peaks: float32 [5, 786432], P(None, ('tm', 'tmpl'))
The draws below stay inside these ranges and needn't reach their ends.
Inputs may be any that keep to these rules, and one draw needn't show every extreme that they name: `bin_edges`: each row holds 15 bin edges in strictly increasing order.
All inputs are finite; a program needn't handle non-finite values. No bound on the sum of `segment_valid` on one device may be relied on, other than what follows from the above.
Results may differ from the reference program's by a relative error of at most 0.0014.
Values sent between devices are 32-bit elements; how exact they have to be, the bound alone decides.
A program may use at most 64 MiB of HBM per device.

```python
import math
import jax
import jax.numpy as jnp
from jax import lax

DET = 2
BLOCK = 1024
TLEN = 512
STRIDE = 512
FBAND = 256
FLOW = 4
BINS = 16
SEG = 256
TEMPLATES = 16
SAMPLES = 786432


def draw_strain(key, part):
    noise_key = jax.random.fold_in(key, 11)
    timeline = jnp.arange(SAMPLES, dtype=jnp.float32) / SAMPLES
    detector_level = 1.0 + 0.4 * jnp.arange(DET, dtype=jnp.float32)[:, None]
    noise = jax.random.normal(noise_key, (DET, SAMPLES + 2), jnp.float32)
    colored = noise[:, 2:] + 0.9 * noise[:, 1:-1] + 0.5 * noise[:, :-2]
    level = 10.0 ** (0.5 * timeline)
    return jnp.clip(colored * level[None, :] * detector_level, -24.0, 24.0)


def draw_bin_edges(key, part):
    row_keys = jax.random.split(jax.random.fold_in(key, 23), TEMPLATES)

    def one_row(row_key):
        chosen = jax.random.permutation(row_key, FBAND - 1)[:BINS - 1] + 1
        return jnp.sort(chosen)
    return jax.vmap(one_row)(row_keys).astype(jnp.int32)


def plant(entries, stream_key, low, largest):
    dims = entries.shape
    index_at = [jax.random.randint(jax.random.fold_in(stream_key, axis), (), 0, dims[axis]) for axis in range(len(dims))]
    entries = entries.at[tuple(index_at)].set(low)
    longest = dims.index(max(dims))
    index_at[longest] = (index_at[longest] + 1) % dims[longest]
    return entries.at[tuple(index_at)].set(largest)


def block_scale(key, shape, pieces, smallest, largest):
    level = 1.0
    for position, blocks in pieces:
        draws = jax.random.uniform(jax.random.fold_in(jax.random.fold_in(key, 6), position), (blocks,), jnp.float32, smallest / len(pieces), largest / len(pieces))
        level = level * jnp.repeat(jnp.exp(draws), shape[position] // blocks).reshape((-1,) + (1,) * (len(shape) - 1 - position))
    return level


def gaussian(own_key, shape, scale, most, cuts=(), kind=jnp.bfloat16):
    array = scale * jax.random.normal(own_key, shape, jnp.float32)
    if cuts:
        array = array * block_scale(own_key, shape, cuts, -0.22, 0.18)
    return jnp.clip(array, -most, most).astype(kind)


def setup_inputs(seed: int = 0) -> dict:
    streams_of = jax.random.split(jax.random.key(seed), 6)
    strain = draw_strain(jax.random.fold_in(streams_of[5], 71), 0)
    segment_valid = plant((jax.random.randint(streams_of[1], (DET, SAMPLES // SEG), 0, 8) < 7).astype(jnp.int32), jax.random.fold_in(streams_of[1], 1), 0, 1)
    templates = gaussian(streams_of[2], (TEMPLATES, TLEN), 1.0, 6.0, ((0, 8),), jnp.float32)
    durations = plant(jax.random.randint(streams_of[3], (TEMPLATES,), TLEN // 4, TLEN + 1), jax.random.fold_in(streams_of[3], 1), TLEN // 4, TLEN).astype(jnp.int32)
    bin_edges = draw_bin_edges(jax.random.fold_in(streams_of[5], 71), 0)
    return dict(strain=strain, segment_valid=segment_valid, templates=templates, durations=durations, bin_edges=bin_edges)


epsilon = 1e-06

def forward_table():
    frequency = FLOW + jnp.arange(FBAND, dtype=jnp.int32)
    sample = jnp.arange(BLOCK, dtype=jnp.int32)
    phase_idx = sample[:, None] * frequency[None, :] % BLOCK
    angles = 2.0 * math.pi / BLOCK * phase_idx.astype(jnp.float32)
    factor = 1.0 / math.sqrt(BLOCK)
    return jnp.concatenate([jnp.cos(angles), -jnp.sin(angles)], axis=1) * factor

def inverse_table():
    frequency = FLOW + jnp.arange(FBAND, dtype=jnp.int32)
    offset = jnp.arange(STRIDE, dtype=jnp.int32)
    phase_idx = frequency[:, None] * offset[None, :] % BLOCK
    angles = 2.0 * math.pi / BLOCK * phase_idx.astype(jnp.float32)
    cosine = jnp.cos(angles)
    sine = jnp.sin(angles)
    upper_rows = jnp.concatenate([cosine, sine], axis=1)
    lower_rows = jnp.concatenate([-sine, cosine], axis=1)
    return jnp.concatenate([upper_rows, lower_rows], axis=0).astype(jnp.bfloat16)

def bin_members(bin_edges):
    band_index = jnp.arange(FBAND, dtype=jnp.int32)
    bin_index = lax.optimization_barrier(jnp.sum((band_index[None, :, None] >= bin_edges[:, None, :]).astype(jnp.int32), axis=2))
    member = bin_index[:, None, :] == jnp.arange(BINS, dtype=jnp.int32)[None, :, None]
    return jnp.concatenate([member, member], axis=2)

def score_templates(spectra, shapes, member, noise_power, inverse):
    real_part = spectra[..., :FBAND]
    imag_part = spectra[..., FBAND:]
    shape_real = shapes[:, :FBAND]
    shape_imag = shapes[:, FBAND:]
    weight = 1.0 / noise_power
    filter_real = shape_real[:, None, :] * weight[None]
    filter_imag = -shape_imag[:, None, :] * weight[None]
    sigma_sq = lax.optimization_barrier(jnp.sum((shape_real * shape_real + shape_imag * shape_imag)[:, None, :] * weight[None], axis=2))
    prod_real = real_part[None] * filter_real[:, :, None, :] - imag_part[None] * filter_imag[:, :, None, :]
    prod_imag = real_part[None] * filter_imag[:, :, None, :] + imag_part[None] * filter_real[:, :, None, :]
    product = jnp.concatenate([prod_real, prod_imag], axis=3).astype(jnp.bfloat16)
    inverse_wide = inverse.astype(jnp.float32)
    initial = jnp.zeros(product.shape[:3] + (2 * STRIDE,), jnp.float32)

    def add_bin(state_pair, in_bin):
        summed, squares = state_pair
        masked = jnp.where(in_bin[:, None, None, :], product, jnp.zeros_like(product)).astype(jnp.float32)
        binned = jnp.einsum('kdnf,fv->kdnv', masked, inverse_wide)
        part_real = binned[..., :STRIDE]
        part_imag = binned[..., STRIDE:]
        return ((summed + binned, squares + part_real * part_real + part_imag * part_imag), None)
    (summed, squares), unused = lax.scan(add_bin, (initial, initial[..., :STRIDE]), jnp.moveaxis(member, 1, 0))
    corr_real = summed[..., :STRIDE]
    corr_imag = summed[..., STRIDE:]
    magnitude = corr_real * corr_real + corr_imag * corr_imag
    sigma_wide = sigma_sq[:, :, None, None]
    strength = jnp.sqrt(magnitude / sigma_wide)
    chi_square = (BINS * squares - magnitude) / sigma_wide
    reduced = jnp.maximum(chi_square / (2.0 * BINS - 2.0), 1.0)
    weighted = strength * ((1.0 + reduced ** 3) / 2.0) ** (-1.0 / 6.0)
    new_shape = (product.shape[0], product.shape[1], product.shape[2] * STRIDE)
    return (strength.reshape(new_shape), weighted.reshape(new_shape))

def peak_rows(strength, weighted):
    network = jnp.sqrt(lax.optimization_barrier(jnp.sum(weighted * weighted, axis=1)))
    return jnp.concatenate([lax.optimization_barrier(jnp.max(strength, axis=0)), lax.optimization_barrier(jnp.max(weighted, axis=0)), lax.optimization_barrier(jnp.max(network, axis=0))[None]], axis=0)

def reference(strain, segment_valid, templates, durations, bin_edges):
    gated_strain = (strain.reshape(DET, -1, SEG) * segment_valid[:, :, None].astype(jnp.float32)).reshape(DET, SAMPLES)
    padded = jnp.concatenate([gated_strain, jnp.zeros((DET, TLEN), jnp.float32)], axis=1)
    block_count = SAMPLES // STRIDE
    first_half = padded[:, :SAMPLES].reshape(DET, block_count, STRIDE)
    second_half = padded[:, STRIDE:SAMPLES + STRIDE].reshape(DET, block_count, STRIDE)
    frames = jnp.concatenate([first_half, second_half], axis=2)
    forward = forward_table()
    spectra = jnp.einsum('dnb,bf->dnf', frames, forward, precision=lax.Precision.HIGHEST)
    squared = lax.optimization_barrier(jnp.sum(spectra * spectra, axis=1))
    noise_power = (squared[:, :FBAND] + squared[:, FBAND:]) / block_count + epsilon
    within = (jnp.arange(TLEN, dtype=jnp.int32)[None, :] < durations[:, None]).astype(jnp.float32)
    shapes = jnp.dot(templates * within, forward[:TLEN], precision=lax.Precision.HIGHEST)
    member = bin_members(bin_edges)
    inverse = inverse_table()

    def advance(highest, member_pair):
        one_shape, one_member = member_pair
        strength, weighted = score_templates(spectra, one_shape[None], one_member[None], noise_power, inverse)
        return (jnp.maximum(highest, peak_rows(strength, weighted)), None)
    highest, unused = lax.scan(advance, jnp.zeros((2 * DET + 1, SAMPLES), jnp.float32), (shapes, member))
    return highest
```

```python
import math

import jax
import jax.numpy as jnp
import numpy as np
from jax import lax
from jax.experimental import pallas as pl
from jax.experimental.pallas import tpu as pltpu
from jax.sharding import PartitionSpec as P

DET = 2
BLOCK = 1024
TLEN = 512
STRIDE = 512
FBAND = 256
FLOW = 4
BINS = 16
SEG = 256
POINTS = 128
NARROW = POINTS // 2
EXTRA = 8
MESH = pl.DeviceIdType.MESH

epsilon = 1e-06


def forward_table():
    frequency = FLOW + np.arange(FBAND)
    phase = np.arange(STRIDE)[:, None] * frequency[None, :] % BLOCK
    angles = np.float32(2.0 * math.pi / BLOCK) * phase.astype(np.float32)
    factor = np.float32(1.0 / math.sqrt(BLOCK))
    return np.concatenate([np.cos(angles), -np.sin(angles)], axis=1) * factor


def rotation_table(frequency, offset, period):
    phase = frequency[:, None] * offset[None, :] % period
    angles = np.float32(2.0 * math.pi / period) * phase.astype(np.float32)
    cosine, sine = np.cos(angles), np.sin(angles)
    upper = np.concatenate([cosine, sine], axis=1)
    lower = np.concatenate([-sine, cosine], axis=1)
    return np.concatenate([upper, lower], axis=0)


def spread_table():
    step = BLOCK // POINTS
    delta = np.arange(STRIDE)[None, :] - step * np.arange(POINTS)[:, None]
    lags = np.arange(1, NARROW)
    waves = np.cos(2.0 * math.pi / BLOCK * (delta[:, :, None] * lags % BLOCK))
    table = (1.0 + 2.0 * waves.sum(axis=2)) / POINTS
    return np.concatenate([table, table], axis=0)


def prepare(n_tm, n_tp, blocks, x_ref, valid_ref, edge_ref, table_ref, spec_ref, filt_ref,
            sig_ref, cut_ref, g_ref, head, halo, pack, part, whole, halo_sem, pack_send,
            pack_recv, part_send, part_recv, whole_send, whole_recv):
    me_tm, me_tp = lax.axis_index("tm"), lax.axis_index("tmpl")
    rows = DET * blocks
    halo[...] = jnp.zeros_like(halo)
    barrier = pltpu.get_barrier_semaphore()
    for r in range(1, n_tp):
        pl.semaphore_signal(barrier, inc=1, device_id=(me_tm, lax.rem(me_tp + r, n_tp)),
                            device_id_type=MESH)
    for r in range(1, n_tm):
        pl.semaphore_signal(barrier, inc=1, device_id=(lax.rem(me_tm + r, n_tm), me_tp),
                            device_id_type=MESH)
    valid = valid_ref[...]
    lane = lax.broadcasted_iota(jnp.int32, x_ref.shape, 1)
    gate = jnp.where(lane < SEG, valid[:, :1], valid[:, 1:2])
    g = jnp.dot(x_ref[...] * gate, table_ref[...], precision=lax.Precision.HIGHEST,
                preferred_element_type=jnp.float32)
    for d in range(DET):
        g_ref[d, :blocks, :] = g[d * blocks:(d + 1) * blocks]
        g_ref[d, blocks:blocks + 1, :] = g[rows + d:rows + d + 1]
    head[...] = g[rows + DET:rows + 2 * DET]
    pack[0, :, :2 * FBAND] = g[rows + 2 * DET:rows + 2 * DET + 2]
    pack[0, :, 2 * FBAND:] = edge_ref[...]
    pl.semaphore_wait(barrier, n_tp + n_tm - 2)

    last = me_tp == n_tp - 1

    def halo_copy():
        return pltpu.make_async_remote_copy(
            src_ref=head, dst_ref=halo, send_sem=halo_sem.at[0], recv_sem=halo_sem.at[1],
            device_id=(lax.rem(me_tm + n_tm - 1, n_tm), me_tp), device_id_type=MESH)

    @pl.when(jnp.logical_and(last, me_tm > 0))
    def _():
        halo_copy().start()

    packs = []
    for r in range(1, n_tp):
        packs.append(pltpu.make_async_remote_copy(
            src_ref=pack.at[0], dst_ref=pack.at[r], send_sem=pack_send.at[r],
            recv_sem=pack_recv.at[r], device_id=(me_tm, lax.rem(me_tp + r, n_tp)),
            device_id_type=MESH))
        packs[-1].start()

    @pl.when(jnp.logical_and(last, me_tm < n_tm - 1))
    def _():
        halo_copy().wait_recv()

    @pl.when(last)
    def _():
        for d in range(DET):
            g_ref[d, blocks:blocks + 1, :] = halo[d:d + 1, :]

    column = lax.broadcasted_iota(jnp.int32, (1, 2 * FBAND), 1)
    sign = jnp.where(column % 2 == 0, 1.0, -1.0)
    for d in range(DET):
        s = g_ref[d, :blocks, :] + sign * g_ref[d, 1:blocks + 1, :]
        spec_ref[d * blocks:(d + 1) * blocks, :] = s
        power = jnp.sum(s * s, axis=0, keepdims=True)
        part[0, d:d + 1, :] = power[:, :FBAND] + power[:, FBAND:]

    parts = []
    for r in range(1, n_tp):
        parts.append(pltpu.make_async_remote_copy(
            src_ref=part.at[0], dst_ref=part.at[r], send_sem=part_send.at[r],
            recv_sem=part_recv.at[r], device_id=(me_tm, lax.rem(me_tp + r, n_tp)),
            device_id_type=MESH))
        parts[-1].start()
    for copy in parts:
        copy.wait_recv()
    total = part[0]
    for r in range(1, n_tp):
        total = total + part[r]
    whole[0] = total
    wholes = []
    for r in range(1, n_tm):
        wholes.append(pltpu.make_async_remote_copy(
            src_ref=whole.at[0], dst_ref=whole.at[r], send_sem=whole_send.at[r],
            recv_sem=whole_recv.at[r], device_id=(lax.rem(me_tm + r, n_tm), me_tp),
            device_id_type=MESH))
        wholes[-1].start()
    for copy in packs:
        copy.wait_recv()
    for copy in wholes:
        copy.wait_recv()
    total = whole[0]
    for r in range(1, n_tm):
        total = total + whole[r]
    weight = 1.0 / (total / (blocks * n_tp * n_tm) + epsilon)
    for r in range(n_tp):
        for i in range(2):
            re, im = pack[r, i:i + 1, :FBAND], pack[r, i:i + 1, FBAND:2 * FBAND]
            filt_ref[2 * r + i, :, :FBAND] = re * weight
            filt_ref[2 * r + i, :, FBAND:] = -im * weight
            sigma = jnp.sum((re * re + im * im) * weight, axis=1, keepdims=True)
            sig_ref[2 * r + i] = jnp.broadcast_to(1.0 / sigma, (DET, 128))
        cut_ref[r] = pack[r, :, 2 * FBAND:].astype(jnp.int32)
    for copy in packs + parts + wholes:
        copy.wait_send()

    @pl.when(jnp.logical_and(last, me_tm > 0))
    def _():
        halo_copy().wait_send()


def score(count, blocks, cut_ref, spec_ref, filt_ref, sig_ref, inverse_ref, sample_ref,
          spread_ref, out_ref, prod, lhs, squares):
    rows = DET * blocks
    out_ref[...] = jnp.zeros_like(out_ref)

    def one(j, carry):
        filt = filt_ref[j]
        for d in range(DET):
            own = slice(d * blocks, (d + 1) * blocks)
            sr, si = spec_ref[own, :FBAND], spec_ref[own, FBAND:]
            fr, fi = filt[d:d + 1, :FBAND], filt[d:d + 1, FBAND:]
            prod[own, :FBAND] = (sr * fr - si * fi).astype(jnp.bfloat16)
            prod[own, FBAND:] = (sr * fi + si * fr).astype(jnp.bfloat16)
        product = prod[...]
        edges = [0] + [cut_ref[j, p] for p in range(BINS - 1)] + [FBAND]
        lane = lax.broadcasted_iota(jnp.int32, (1, 128), 1)
        widest = 0
        for p in range(BINS):
            low, high = edges[p], edges[p + 1]
            widest = jnp.maximum(widest, high - low)
            high = jnp.where(high - low > NARROW, low, high)
            masks = [
                jnp.where((lane + k >= low) & (lane + k < high), 1.0, 0.0).astype(jnp.bfloat16)
                for k in (0, 128)
            ]
            part = slice(p * rows, (p + 1) * rows)
            lhs[part, :128] = product[:, :128] * masks[0] + product[:, 128:256] * masks[1]
            lhs[part, 128:] = product[:, 256:384] * masks[0] + product[:, 384:] * masks[1]
        points = jnp.dot(lhs[...], sample_ref[...], preferred_element_type=jnp.float32)
        points = points * points
        points = (points[:, :POINTS] + points[:, POINTS:]).reshape(BINS, rows, POINTS)
        total = jnp.sum(points, axis=0)
        upper = total.astype(jnp.bfloat16)
        lower = (total - upper.astype(jnp.float32)).astype(jnp.bfloat16)
        squares[...] = jnp.dot(jnp.concatenate([upper, lower], axis=1), spread_ref[...],
                               preferred_element_type=jnp.float32)

        @pl.when(widest > NARROW)
        def _():
            def one_bin(p, carry):
                low = jnp.where(p == 0, 0, cut_ref[j, jnp.maximum(p - 1, 0)])
                high = jnp.where(p == BINS - 1, FBAND, cut_ref[j, jnp.minimum(p, BINS - 2)])

                @pl.when(high - low > NARROW)
                def _():
                    column = lax.broadcasted_iota(jnp.int32, (1, 2 * FBAND), 1) % FBAND
                    mask = jnp.where((column >= low) & (column < high), 1.0, 0.0)
                    masked = prod[...] * mask.astype(jnp.bfloat16)
                    z = jnp.dot(masked, inverse_ref[...], preferred_element_type=jnp.float32)
                    z = z * z
                    squares[...] += z[:, :STRIDE] + z[:, STRIDE:]

                return carry

            lax.fori_loop(0, BINS, one_bin, 0)

        corr = jnp.dot(product, inverse_ref[...], preferred_element_type=jnp.float32)
        corr = corr * corr
        magnitude = corr[:, :STRIDE] + corr[:, STRIDE:]
        network = None
        for d in range(DET):
            own = slice(d * blocks, (d + 1) * blocks)
            scale = sig_ref[j][d:d + 1, :1]
            mag = magnitude[own]
            strength = mag * scale
            reduced = (BINS * squares[own, :] - mag) * (scale * (1.0 / (2.0 * BINS - 2.0)))
            reduced = jnp.maximum(reduced, 1.0)
            half = 0.5 + 0.5 * (reduced * reduced * reduced)
            weighted = strength * jnp.exp2(jnp.log2(half) * (-1.0 / 3.0))
            out_ref[d] = jnp.maximum(out_ref[d], strength)
            out_ref[DET + d] = jnp.maximum(out_ref[DET + d], weighted)
            network = weighted if network is None else network + weighted
        out_ref[2 * DET] = jnp.maximum(out_ref[2 * DET], network)
        return carry

    lax.fori_loop(0, count, one, 0)
    out_ref[...] = jnp.sqrt(out_ref[...])


def shards(strain, segment_valid, templates, durations, bin_edges):
    n_tm, n_tp = lax.axis_size("tm"), lax.axis_size("tmpl")
    me_tp = lax.axis_index("tmpl")
    span_len = strain.shape[1]
    piece = span_len // n_tp
    blocks = piece // STRIDE
    rows = DET * blocks
    per = templates.shape[0]
    count = per * n_tp
    pick = STRIDE // SEG

    start = me_tp * piece
    follow = lax.rem(me_tp + 1, n_tp) * piece
    own = lax.dynamic_slice_in_dim(strain, start, piece, 1).reshape(rows, STRIDE)
    next_block = lax.dynamic_slice_in_dim(strain, follow, STRIDE, 1)
    within = jnp.arange(TLEN, dtype=jnp.int32)[None, :] < durations[:, None]
    shaped = jnp.where(within, templates, 0.0)
    spare = EXTRA - 2 * DET - per
    x = jnp.concatenate(
        [own, next_block, strain[:, :STRIDE], shaped, jnp.zeros((spare, STRIDE), jnp.float32)])
    own_valid = lax.dynamic_slice_in_dim(segment_valid, start // SEG, pick * blocks, 1)
    next_valid = lax.dynamic_slice_in_dim(segment_valid, follow // SEG, pick, 1)
    valid = jnp.concatenate(
        [own_valid.reshape(rows, pick), next_valid, segment_valid[:, :pick],
         jnp.ones((per + spare, pick), jnp.int32)]).astype(jnp.float32)
    edges = jnp.pad(bin_edges.astype(jnp.float32), ((0, 0), (0, 128 - bin_edges.shape[1])))

    vmem = pl.BlockSpec(memory_space=pltpu.VMEM)
    smem = pl.BlockSpec(memory_space=pltpu.SMEM)
    dma = pltpu.SemaphoreType.DMA
    f32 = jnp.float32

    def body(*refs):
        prepare(n_tm, n_tp, blocks, *refs)

    spec, filt, sig, cut = pl.pallas_call(
        body,
        out_shape=(
            jax.ShapeDtypeStruct((rows, 2 * FBAND), f32),
            jax.ShapeDtypeStruct((count, DET, 2 * FBAND), f32),
            jax.ShapeDtypeStruct((count, DET, 128), f32),
            jax.ShapeDtypeStruct((n_tp, per, 128), jnp.int32),
        ),
        in_specs=[vmem] * 4,
        out_specs=(vmem,) * 4,
        scratch_shapes=[
            pltpu.VMEM((DET, blocks + 8, 2 * FBAND), f32),
            pltpu.VMEM((DET, 2 * FBAND), f32),
            pltpu.VMEM((DET, 2 * FBAND), f32),
            pltpu.VMEM((n_tp, per, 2 * FBAND + 128), f32),
            pltpu.VMEM((n_tp, DET, FBAND), f32),
            pltpu.VMEM((n_tm, DET, FBAND), f32),
            dma((2,)), dma((n_tp,)), dma((n_tp,)), dma((n_tp,)), dma((n_tp,)),
            dma((n_tm,)), dma((n_tm,)),
        ],
        compiler_params=pltpu.CompilerParams(
            collective_id=0, has_side_effects=True, vmem_limit_bytes=40 * 2**20),
    )(x, valid, edges, jnp.asarray(forward_table()))

    inverse = rotation_table(FLOW + np.arange(FBAND), np.arange(STRIDE), BLOCK)
    sample = rotation_table(np.arange(POINTS), np.arange(POINTS), POINTS)
    as_bf16 = lambda table: jnp.asarray(table.astype(jnp.bfloat16))

    def scoring(*refs):
        score(count, blocks, *refs)

    out = pl.pallas_call(
        scoring,
        out_shape=jax.ShapeDtypeStruct((2 * DET + 1, blocks, STRIDE), f32),
        in_specs=[smem] + [vmem] * 6,
        out_specs=vmem,
        scratch_shapes=[
            pltpu.VMEM((rows, 2 * FBAND), jnp.bfloat16),
            pltpu.VMEM((BINS * rows, 2 * POINTS), jnp.bfloat16),
            pltpu.VMEM((rows, STRIDE), f32),
        ],
        compiler_params=pltpu.CompilerParams(vmem_limit_bytes=40 * 2**20),
    )(cut.reshape(count, 128)[:, :BINS], spec, filt, sig, as_bf16(inverse), as_bf16(sample),
      as_bf16(spread_table()))
    return out.reshape(2 * DET + 1, piece)


def solution(mesh):
    placed = (P(None, "tm"), P(None, "tm"), P("tmpl", None), P("tmpl"), P("tmpl", None))
    return jax.shard_map(
        shards, mesh=mesh, in_specs=placed, out_specs=P(None, ("tm", "tmpl")), check_vma=False
    )
```

```python
import math

import jax
import jax.numpy as jnp
import numpy as np
from jax import lax
from jax.experimental import pallas as pl
from jax.experimental.pallas import tpu as pltpu
from jax.sharding import PartitionSpec as P

DET = 2
BLOCK = 1024
TLEN = 512
STRIDE = 512
FBAND = 256
FLOW = 4
BINS = 16
SEG = 256
POINTS = 128
NARROW = POINTS // 2
EXTRA = 8
GROUP = 4
MESH = pl.DeviceIdType.MESH

epsilon = 1e-06


def forward_table():
    frequency = FLOW + np.arange(FBAND)
    phase = np.arange(STRIDE)[:, None] * frequency[None, :] % BLOCK
    angles = np.float32(2.0 * math.pi / BLOCK) * phase.astype(np.float32)
    factor = np.float32(1.0 / math.sqrt(BLOCK))
    return np.concatenate([np.cos(angles), -np.sin(angles)], axis=1) * factor


def rotation_table(frequency, offset, period):
    phase = frequency[:, None] * offset[None, :] % period
    angles = np.float32(2.0 * math.pi / period) * phase.astype(np.float32)
    cosine, sine = np.cos(angles), np.sin(angles)
    upper = np.concatenate([cosine, sine], axis=1)
    lower = np.concatenate([-sine, cosine], axis=1)
    return np.concatenate([upper, lower], axis=0)


def spread_table():
    step = BLOCK // POINTS
    delta = np.arange(STRIDE)[None, :] - step * np.arange(POINTS)[:, None]
    lags = np.arange(1, NARROW)
    waves = np.cos(2.0 * math.pi / BLOCK * (delta[:, :, None] * lags % BLOCK))
    table = (1.0 + 2.0 * waves.sum(axis=2)) / POINTS
    return np.concatenate([table, table], axis=0)


def prepare(n_tm, n_tp, blocks, x_ref, valid_ref, edge_ref, table_ref, spec_ref, filt_ref,
            sig_ref, cut_ref, g_ref, head, halo, pack, part, whole, halo_sem, pack_send,
            pack_recv, part_send, part_recv, whole_send, whole_recv):
    me_tm, me_tp = lax.axis_index("tm"), lax.axis_index("tmpl")
    rows = DET * blocks
    halo[...] = jnp.zeros_like(halo)
    barrier = pltpu.get_barrier_semaphore()
    for r in range(1, n_tp):
        pl.semaphore_signal(barrier, inc=1, device_id=(me_tm, lax.rem(me_tp + r, n_tp)),
                            device_id_type=MESH)
    for r in range(1, n_tm):
        pl.semaphore_signal(barrier, inc=1, device_id=(lax.rem(me_tm + r, n_tm), me_tp),
                            device_id_type=MESH)
    valid = valid_ref[...]
    lane = lax.broadcasted_iota(jnp.int32, x_ref.shape, 1)
    gate = jnp.where(lane < SEG, valid[:, :1], valid[:, 1:2])
    g = jnp.dot(x_ref[...] * gate, table_ref[...], precision=lax.Precision.HIGHEST,
                preferred_element_type=jnp.float32)
    for d in range(DET):
        g_ref[d, :blocks, :] = g[d * blocks:(d + 1) * blocks]
        g_ref[d, blocks:blocks + 1, :] = g[rows + d:rows + d + 1]
    head[...] = g[rows + DET:rows + 2 * DET]
    pack[0, :, :2 * FBAND] = g[rows + 2 * DET:rows + 2 * DET + 2]
    pack[0, :, 2 * FBAND:] = edge_ref[...]
    pl.semaphore_wait(barrier, n_tp + n_tm - 2)

    last = me_tp == n_tp - 1

    def halo_copy():
        return pltpu.make_async_remote_copy(
            src_ref=head, dst_ref=halo, send_sem=halo_sem.at[0], recv_sem=halo_sem.at[1],
            device_id=(lax.rem(me_tm + n_tm - 1, n_tm), me_tp), device_id_type=MESH)

    @pl.when(jnp.logical_and(last, me_tm > 0))
    def _():
        halo_copy().start()

    packs = []
    for r in range(1, n_tp):
        packs.append(pltpu.make_async_remote_copy(
            src_ref=pack.at[0], dst_ref=pack.at[r], send_sem=pack_send.at[r],
            recv_sem=pack_recv.at[r], device_id=(me_tm, lax.rem(me_tp + r, n_tp)),
            device_id_type=MESH))
        packs[-1].start()

    @pl.when(jnp.logical_and(last, me_tm < n_tm - 1))
    def _():
        halo_copy().wait_recv()

    @pl.when(last)
    def _():
        for d in range(DET):
            g_ref[d, blocks:blocks + 1, :] = halo[d:d + 1, :]

    column = lax.broadcasted_iota(jnp.int32, (1, 2 * FBAND), 1)
    sign = jnp.where(column % 2 == 0, 1.0, -1.0)
    for d in range(DET):
        s = g_ref[d, :blocks, :] + sign * g_ref[d, 1:blocks + 1, :]
        spec_ref[d * blocks:(d + 1) * blocks, :] = s
        power = jnp.sum(s * s, axis=0, keepdims=True)
        part[0, d:d + 1, :] = power[:, :FBAND] + power[:, FBAND:]

    parts = []
    for r in range(1, n_tp):
        parts.append(pltpu.make_async_remote_copy(
            src_ref=part.at[0], dst_ref=part.at[r], send_sem=part_send.at[r],
            recv_sem=part_recv.at[r], device_id=(me_tm, lax.rem(me_tp + r, n_tp)),
            device_id_type=MESH))
        parts[-1].start()
    for copy in parts:
        copy.wait_recv()
    total = part[0]
    for r in range(1, n_tp):
        total = total + part[r]
    whole[0] = total
    wholes = []
    for r in range(1, n_tm):
        wholes.append(pltpu.make_async_remote_copy(
            src_ref=whole.at[0], dst_ref=whole.at[r], send_sem=whole_send.at[r],
            recv_sem=whole_recv.at[r], device_id=(lax.rem(me_tm + r, n_tm), me_tp),
            device_id_type=MESH))
        wholes[-1].start()
    for copy in packs:
        copy.wait_recv()
    for copy in wholes:
        copy.wait_recv()
    total = whole[0]
    for r in range(1, n_tm):
        total = total + whole[r]
    weight = 1.0 / (total / (blocks * n_tp * n_tm) + epsilon)
    for r in range(n_tp):
        for i in range(2):
            re, im = pack[r, i:i + 1, :FBAND], pack[r, i:i + 1, FBAND:2 * FBAND]
            filt_ref[2 * r + i, :, :FBAND] = re * weight
            filt_ref[2 * r + i, :, FBAND:] = -im * weight
            sigma = jnp.sum((re * re + im * im) * weight, axis=1, keepdims=True)
            sig_ref[2 * r + i] = jnp.broadcast_to(1.0 / sigma, (DET, 128))
        cut_ref[r] = pack[r, :, 2 * FBAND:].astype(jnp.int32)
    for copy in packs + parts + wholes:
        copy.wait_send()

    @pl.when(jnp.logical_and(last, me_tm > 0))
    def _():
        halo_copy().wait_send()


def score(count, blocks, cut_ref, spec_ref, filt_ref, sig_ref, inverse_ref, sample_ref,
          spread_ref, out_ref, prod, lhs, best, squares_a, squares_b, mag_a, mag_b, turned):
    rows = DET * blocks
    best[...] = jnp.zeros_like(best)

    def fill(j, g):
        filt = filt_ref[j]
        for d in range(DET):
            own = slice(d * blocks, (d + 1) * blocks)
            to = slice(g * rows + d * blocks, g * rows + (d + 1) * blocks)
            sr, si = spec_ref[own, :FBAND], spec_ref[own, FBAND:]
            fr, fi = filt[d:d + 1, :FBAND], filt[d:d + 1, FBAND:]
            prod[to, :FBAND] = (sr * fr - si * fi).astype(jnp.bfloat16)
            prod[to, FBAND:] = (sr * fi + si * fr).astype(jnp.bfloat16)
        product = prod[g * rows:(g + 1) * rows, :]
        edges = [0] + [cut_ref[j, p] for p in range(BINS - 1)] + [FBAND]
        lane = lax.broadcasted_iota(jnp.int32, (16, 128), 1)
        copies = rows // 16
        widest = 0
        for p in range(BINS):
            low, high = edges[p], edges[p + 1]
            widest = jnp.maximum(widest, high - low)
            high = jnp.where(high - low > NARROW, low, high)
            masks = [
                jnp.where((lane + k >= low) & (lane + k < high), 1.0, 0.0).astype(jnp.bfloat16)
                for k in (0, 128)
            ]
            masks = [jnp.concatenate([mask] * copies, axis=0) for mask in masks]
            part = slice((p * GROUP + g) * rows, (p * GROUP + g + 1) * rows)
            lhs[part, :128] = product[:, :128] * masks[0] + product[:, 128:256] * masks[1]
            lhs[part, 128:] = product[:, 256:384] * masks[0] + product[:, 384:] * masks[1]
        return widest

    def produce(j, squares, mag):
        widest = []
        for g in range(GROUP):
            widest.append(fill(j + g, g))
        product = prod[...]
        corr = jnp.dot(product, inverse_ref[...], preferred_element_type=jnp.float32)
        corr = corr * corr
        mag[...] = corr[:, :STRIDE] + corr[:, STRIDE:]
        points = jnp.dot(lhs[...], sample_ref[...], preferred_element_type=jnp.float32)
        points = points * points
        points = (points[:, :POINTS] + points[:, POINTS:]).reshape(BINS, GROUP * rows, POINTS)
        total = jnp.sum(points, axis=0)
        upper = total.astype(jnp.bfloat16)
        lower = (total - upper.astype(jnp.float32)).astype(jnp.bfloat16)
        squares[...] = jnp.dot(jnp.concatenate([upper, lower], axis=1), spread_ref[...],
                               preferred_element_type=jnp.float32)
        return widest

    def add_wide(j, widest, squares):
        for g in range(GROUP):
            own = slice(g * rows, (g + 1) * rows)

            @pl.when(widest[g] > NARROW)
            def _():
                def one_bin(p, carry):
                    low = jnp.where(p == 0, 0, cut_ref[j + g, jnp.maximum(p - 1, 0)])
                    high = jnp.where(
                        p == BINS - 1, FBAND, cut_ref[j + g, jnp.minimum(p, BINS - 2)])

                    @pl.when(high - low > NARROW)
                    def _():
                        column = lax.broadcasted_iota(jnp.int32, (1, 2 * FBAND), 1) % FBAND
                        mask = jnp.where((column >= low) & (column < high), 1.0, 0.0)
                        masked = prod[own, :] * mask.astype(jnp.bfloat16)
                        z = jnp.dot(masked, inverse_ref[...], preferred_element_type=jnp.float32)
                        z = z * z
                        squares[own, :] += BINS * (z[:, :STRIDE] + z[:, STRIDE:])

                    return carry

                lax.fori_loop(0, BINS, one_bin, 0)

    def consume(j, squares, mag):
        for g in range(GROUP):
            network = None
            for d in range(DET):
                own = slice(g * rows + d * blocks, g * rows + (d + 1) * blocks)
                scale = sig_ref[j + g][d:d + 1, :1]
                strength = mag[own, :] * scale
                reduced = (squares[own, :] - mag[own, :]) * (scale * (1.0 / (2.0 * BINS - 2.0)))
                reduced = jnp.maximum(reduced, 1.0)
                cube = reduced * reduced * reduced + 1.0
                weighted = strength * jnp.exp2(jnp.log(cube) * (-1.0 / (3.0 * math.log(2.0))))
                best[d] = jnp.maximum(best[d], strength)
                best[DET + d] = jnp.maximum(best[DET + d], weighted)
                network = weighted if network is None else network + weighted
            best[2 * DET] = jnp.maximum(best[2 * DET], network)

    def step(i, now, later):
        consume(i * GROUP, *now)
        widest = produce((i + 1) * GROUP, *later)
        add_wide((i + 1) * GROUP, widest, later[0])

    slot_a, slot_b = (squares_a, mag_a), (squares_b, mag_b)
    add_wide(0, produce(0, *slot_a), squares_a)

    def pair(i, carry):
        step(2 * i, slot_a, slot_b)
        step(2 * i + 1, slot_b, slot_a)
        return carry

    groups = count // GROUP
    lax.fori_loop(0, (groups - 1) // 2, pair, 0)
    if groups % 2 == 0:
        step(groups - 2, slot_a, slot_b)
        consume(count - GROUP, *slot_b)
    else:
        consume(count - GROUP, *slot_a)
    for d in range(2 * DET + 1):
        gain = 1.0 if d < DET else 2.0 ** (1.0 / 6.0)
        root = jnp.sqrt(best[d]) * gain
        for c in range(STRIDE // 128):
            turned[c, pl.ds(d, blocks, stride=8), :] = root[:, c * 128:(c + 1) * 128]
    for b in range(blocks):
        for c in range(STRIDE // 128):
            at = b * STRIDE + c * 128
            out_ref[:, at:at + 128] = turned[c, 8 * b:8 * b + 2 * DET + 1, :]


def scoring_call(count, blocks):
    f32 = jnp.float32
    rows = DET * blocks
    vmem = pl.BlockSpec(memory_space=pltpu.VMEM)

    def scoring(*refs):
        score(count, blocks, *refs)

    return pl.pallas_call(
        scoring,
        out_shape=jax.ShapeDtypeStruct((2 * DET + 1, blocks * STRIDE), f32),
        in_specs=[pl.BlockSpec(memory_space=pltpu.SMEM)] + [vmem] * 6,
        out_specs=vmem,
        scratch_shapes=[
            pltpu.VMEM((GROUP * rows, 2 * FBAND), jnp.bfloat16),
            pltpu.VMEM((BINS * GROUP * rows, 2 * POINTS), jnp.bfloat16),
            pltpu.VMEM((2 * DET + 1, blocks, STRIDE), f32),
            pltpu.VMEM((GROUP * rows, STRIDE), f32), pltpu.VMEM((GROUP * rows, STRIDE), f32),
            pltpu.VMEM((GROUP * rows, STRIDE), f32), pltpu.VMEM((GROUP * rows, STRIDE), f32),
            pltpu.VMEM((STRIDE // 128, 8 * blocks, 128), f32),
        ],
        compiler_params=pltpu.CompilerParams(vmem_limit_bytes=40 * 2**20),
    )


def scoring_tables():
    inverse = rotation_table(FLOW + np.arange(FBAND), np.arange(STRIDE), BLOCK)
    sample = rotation_table(np.arange(POINTS), np.arange(POINTS), POINTS)
    spread = BINS * spread_table()
    return [jnp.asarray(table.astype(jnp.bfloat16)) for table in (inverse, sample, spread)]


def shards(strain, segment_valid, templates, durations, bin_edges):
    n_tm, n_tp = lax.axis_size("tm"), lax.axis_size("tmpl")
    me_tp = lax.axis_index("tmpl")
    span_len = strain.shape[1]
    piece = span_len // n_tp
    blocks = piece // STRIDE
    rows = DET * blocks
    per = templates.shape[0]
    count = per * n_tp
    pick = STRIDE // SEG

    start = me_tp * piece
    follow = lax.rem(me_tp + 1, n_tp) * piece
    own = lax.dynamic_slice_in_dim(strain, start, piece, 1).reshape(rows, STRIDE)
    next_block = lax.dynamic_slice_in_dim(strain, follow, STRIDE, 1)
    within = jnp.arange(TLEN, dtype=jnp.int32)[None, :] < durations[:, None]
    shaped = jnp.where(within, templates, 0.0)
    spare = EXTRA - 2 * DET - per
    x = jnp.concatenate(
        [own, next_block, strain[:, :STRIDE], shaped, jnp.zeros((spare, STRIDE), jnp.float32)])
    own_valid = lax.dynamic_slice_in_dim(segment_valid, start // SEG, pick * blocks, 1)
    next_valid = lax.dynamic_slice_in_dim(segment_valid, follow // SEG, pick, 1)
    valid = jnp.concatenate(
        [own_valid.reshape(rows, pick), next_valid, segment_valid[:, :pick],
         jnp.ones((per + spare, pick), jnp.int32)]).astype(jnp.float32)
    edges = jnp.pad(bin_edges.astype(jnp.float32), ((0, 0), (0, 128 - bin_edges.shape[1])))

    vmem = pl.BlockSpec(memory_space=pltpu.VMEM)
    dma = pltpu.SemaphoreType.DMA
    f32 = jnp.float32

    def body(*refs):
        prepare(n_tm, n_tp, blocks, *refs)

    spec, filt, sig, cut = pl.pallas_call(
        body,
        out_shape=(
            jax.ShapeDtypeStruct((rows, 2 * FBAND), f32),
            jax.ShapeDtypeStruct((count, DET, 2 * FBAND), f32),
            jax.ShapeDtypeStruct((count, DET, 128), f32),
            jax.ShapeDtypeStruct((n_tp, per, 128), jnp.int32),
        ),
        in_specs=[vmem] * 4,
        out_specs=(vmem,) * 4,
        scratch_shapes=[
            pltpu.VMEM((DET, blocks + 8, 2 * FBAND), f32),
            pltpu.VMEM((DET, 2 * FBAND), f32),
            pltpu.VMEM((DET, 2 * FBAND), f32),
            pltpu.VMEM((n_tp, per, 2 * FBAND + 128), f32),
            pltpu.VMEM((n_tp, DET, FBAND), f32),
            pltpu.VMEM((n_tm, DET, FBAND), f32),
            dma((2,)), dma((n_tp,)), dma((n_tp,)), dma((n_tp,)), dma((n_tp,)),
            dma((n_tm,)), dma((n_tm,)),
        ],
        compiler_params=pltpu.CompilerParams(
            collective_id=0, has_side_effects=True, vmem_limit_bytes=40 * 2**20),
    )(x, valid, edges, jnp.asarray(forward_table()))

    return scoring_call(count, blocks)(
        cut.reshape(count, 128)[:, :BINS], spec, filt, sig, *scoring_tables())


def solution(mesh):
    placed = (P(None, "tm"), P(None, "tm"), P("tmpl", None), P("tmpl"), P("tmpl", None))
    return jax.shard_map(
        shards, mesh=mesh, in_specs=placed, out_specs=P(None, ("tm", "tmpl")), check_vma=False
    )
```

```python
import math

import jax
import jax.numpy as jnp
import numpy as np
from jax import lax
from jax.experimental import pallas as pl
from jax.experimental.pallas import tpu as pltpu
from jax.sharding import PartitionSpec as P

DET = 2
BLOCK = 1024
TLEN = 512
STRIDE = 512
FBAND = 256
FLOW = 4
BINS = 16
SEG = 256
POINTS = 128
NARROW = POINTS // 2
EXTRA = 16
GROUP = 4
MESH = pl.DeviceIdType.MESH

epsilon = 1e-06


def forward_table():
    frequency = FLOW + np.arange(FBAND)
    phase = np.arange(STRIDE)[:, None] * frequency[None, :] % BLOCK
    angles = np.float32(2.0 * math.pi / BLOCK) * phase.astype(np.float32)
    factor = np.float32(1.0 / math.sqrt(BLOCK))
    return np.concatenate([np.cos(angles), -np.sin(angles)], axis=1) * factor


def split_table(table):
    upper = table.astype(jnp.bfloat16)
    lower = (table - upper.astype(np.float32)).astype(jnp.bfloat16)
    return np.stack([upper, lower])


def rotation_table(frequency, offset, period):
    phase = frequency[:, None] * offset[None, :] % period
    angles = np.float32(2.0 * math.pi / period) * phase.astype(np.float32)
    cosine, sine = np.cos(angles), np.sin(angles)
    upper = np.concatenate([cosine, sine], axis=1)
    lower = np.concatenate([-sine, cosine], axis=1)
    return np.concatenate([upper, lower], axis=0)


def spread_table():
    step = BLOCK // POINTS
    delta = np.arange(STRIDE)[None, :] - step * np.arange(POINTS)[:, None]
    lags = np.arange(1, NARROW)
    waves = np.cos(2.0 * math.pi / BLOCK * (delta[:, :, None] * lags % BLOCK))
    table = (1.0 + 2.0 * waves.sum(axis=2)) / POINTS
    return np.concatenate([table, table], axis=0)


def prepare(n_tm, n_tp, blocks, x_ref, valid_ref, edge_ref, table_ref, spec_ref, filt_ref,
            sig_ref, cut_ref, g_ref, head, halo, pack, part, whole, halo_sem, pack_send,
            pack_recv, part_send, part_recv, whole_send, whole_recv):
    me_tm, me_tp = lax.axis_index("tm"), lax.axis_index("tmpl")
    rows = DET * blocks
    halo[...] = jnp.zeros_like(halo)
    barrier = pltpu.get_barrier_semaphore()
    for r in range(1, n_tp):
        pl.semaphore_signal(barrier, inc=1, device_id=(me_tm, lax.rem(me_tp + r, n_tp)),
                            device_id_type=MESH)
    for r in range(1, n_tm):
        pl.semaphore_signal(barrier, inc=1, device_id=(lax.rem(me_tm + r, n_tm), me_tp),
                            device_id_type=MESH)
    valid = valid_ref[...]
    lane = lax.broadcasted_iota(jnp.int32, x_ref.shape, 1)
    gate = jnp.where(lane < SEG, valid[:, :1], valid[:, 1:2])
    gated = x_ref[...] * gate
    upper = gated.astype(jnp.bfloat16)
    lower = (gated - upper.astype(jnp.float32)).astype(jnp.bfloat16)
    g = jnp.dot(upper, table_ref[0], preferred_element_type=jnp.float32)
    g += jnp.dot(upper, table_ref[1], preferred_element_type=jnp.float32)
    g += jnp.dot(lower, table_ref[0], preferred_element_type=jnp.float32)
    for d in range(DET):
        g_ref[d, :blocks, :] = g[d * blocks:(d + 1) * blocks]
        g_ref[d, blocks:blocks + 1, :] = g[rows + d:rows + d + 1]
    head[...] = g[rows + DET:rows + 2 * DET]
    pack[0, :, :2 * FBAND] = g[rows + 2 * DET:rows + 2 * DET + 2]
    pack[0, :, 2 * FBAND:] = edge_ref[...]
    pl.semaphore_wait(barrier, n_tp + n_tm - 2)

    last = me_tp == n_tp - 1

    def halo_copy():
        return pltpu.make_async_remote_copy(
            src_ref=head, dst_ref=halo, send_sem=halo_sem.at[0], recv_sem=halo_sem.at[1],
            device_id=(lax.rem(me_tm + n_tm - 1, n_tm), me_tp), device_id_type=MESH)

    @pl.when(jnp.logical_and(last, me_tm > 0))
    def _():
        halo_copy().start()

    packs = []
    for r in range(1, n_tp):
        packs.append(pltpu.make_async_remote_copy(
            src_ref=pack.at[0], dst_ref=pack.at[r], send_sem=pack_send.at[r],
            recv_sem=pack_recv.at[r], device_id=(me_tm, lax.rem(me_tp + r, n_tp)),
            device_id_type=MESH))
        packs[-1].start()

    @pl.when(jnp.logical_and(last, me_tm < n_tm - 1))
    def _():
        halo_copy().wait_recv()

    @pl.when(last)
    def _():
        for d in range(DET):
            g_ref[d, blocks:blocks + 1, :] = halo[d:d + 1, :]

    column = lax.broadcasted_iota(jnp.int32, (1, 2 * FBAND), 1)
    sign = jnp.where(column % 2 == 0, 1.0, -1.0)
    for d in range(DET):
        s = g_ref[d, :blocks, :] + sign * g_ref[d, 1:blocks + 1, :]
        spec_ref[d * blocks:(d + 1) * blocks, :] = s
        power = jnp.sum(s * s, axis=0, keepdims=True)
        part[0, d:d + 1, :] = power[:, :FBAND] + power[:, FBAND:]

    parts = []
    for r in range(1, n_tp):
        parts.append(pltpu.make_async_remote_copy(
            src_ref=part.at[0], dst_ref=part.at[r], send_sem=part_send.at[r],
            recv_sem=part_recv.at[r], device_id=(me_tm, lax.rem(me_tp + r, n_tp)),
            device_id_type=MESH))
        parts[-1].start()
    for copy in parts:
        copy.wait_recv()
    total = part[0]
    for r in range(1, n_tp):
        total = total + part[r]
    whole[0] = total
    wholes = []
    for r in range(1, n_tm):
        wholes.append(pltpu.make_async_remote_copy(
            src_ref=whole.at[0], dst_ref=whole.at[r], send_sem=whole_send.at[r],
            recv_sem=whole_recv.at[r], device_id=(lax.rem(me_tm + r, n_tm), me_tp),
            device_id_type=MESH))
        wholes[-1].start()
    for copy in packs:
        copy.wait_recv()
    for copy in wholes:
        copy.wait_recv()
    total = whole[0]
    for r in range(1, n_tm):
        total = total + whole[r]
    weight = 1.0 / (total / (blocks * n_tp * n_tm) + epsilon)
    for r in range(n_tp):
        for i in range(2):
            re, im = pack[r, i:i + 1, :FBAND], pack[r, i:i + 1, FBAND:2 * FBAND]
            filt_ref[2 * r + i, :, :FBAND] = re * weight
            filt_ref[2 * r + i, :, FBAND:] = -im * weight
            sigma = jnp.sum((re * re + im * im) * weight, axis=1, keepdims=True)
            sig_ref[2 * r + i] = jnp.broadcast_to(1.0 / sigma, (DET, 128))
        cut_ref[r] = pack[r, :, 2 * FBAND:].astype(jnp.int32)
    for copy in packs + parts + wholes:
        copy.wait_send()

    @pl.when(jnp.logical_and(last, me_tm > 0))
    def _():
        halo_copy().wait_send()


def score(count, blocks, cut_ref, spec_ref, filt_ref, sig_ref, inverse_ref, sample_ref,
          spread_ref, out_ref, prod, lhs, best, squares_a, squares_b, mag_a, mag_b, turned):
    rows = DET * blocks
    best[...] = jnp.zeros_like(best)

    def fill(j, g):
        filt = filt_ref[j]
        for d in range(DET):
            own = slice(d * blocks, (d + 1) * blocks)
            to = slice(g * rows + d * blocks, g * rows + (d + 1) * blocks)
            sr, si = spec_ref[own, :FBAND], spec_ref[own, FBAND:]
            fr, fi = filt[d:d + 1, :FBAND], filt[d:d + 1, FBAND:]
            prod[to, :FBAND] = (sr * fr - si * fi).astype(jnp.bfloat16)
            prod[to, FBAND:] = (sr * fi + si * fr).astype(jnp.bfloat16)
        product = prod[g * rows:(g + 1) * rows, :]
        edges = [0] + [cut_ref[j, p] for p in range(BINS - 1)] + [FBAND]
        lane = lax.broadcasted_iota(jnp.int32, (16, 128), 1)
        copies = rows // 16
        widest = 0
        for p in range(BINS):
            low, high = edges[p], edges[p + 1]
            widest = jnp.maximum(widest, high - low)
            high = jnp.where(high - low > NARROW, low, high)
            masks = [
                jnp.where((lane + k >= low) & (lane + k < high), 1.0, 0.0).astype(jnp.bfloat16)
                for k in (0, 128)
            ]
            masks = [jnp.concatenate([mask] * copies, axis=0) for mask in masks]
            part = slice((p * GROUP + g) * rows, (p * GROUP + g + 1) * rows)
            lhs[part, :128] = product[:, :128] * masks[0] + product[:, 128:256] * masks[1]
            lhs[part, 128:] = product[:, 256:384] * masks[0] + product[:, 384:] * masks[1]
        return widest

    def produce(j, squares, mag):
        widest = []
        for g in range(GROUP):
            widest.append(fill(j + g, g))
        product = prod[...]
        corr = jnp.dot(product, inverse_ref[...], preferred_element_type=jnp.float32)
        corr = corr * corr
        mag[...] = corr[:, :STRIDE] + corr[:, STRIDE:]
        points = jnp.dot(lhs[...], sample_ref[...], preferred_element_type=jnp.float32)
        points = points * points
        points = (points[:, :POINTS] + points[:, POINTS:]).reshape(BINS, GROUP * rows, POINTS)
        total = jnp.sum(points, axis=0)
        upper = total.astype(jnp.bfloat16)
        lower = (total - upper.astype(jnp.float32)).astype(jnp.bfloat16)
        squares[...] = jnp.dot(jnp.concatenate([upper, lower], axis=1), spread_ref[...],
                               preferred_element_type=jnp.float32)
        return widest

    def add_wide(j, widest, squares):
        for g in range(GROUP):
            own = slice(g * rows, (g + 1) * rows)

            @pl.when(widest[g] > NARROW)
            def _():
                def one_bin(p, carry):
                    low = jnp.where(p == 0, 0, cut_ref[j + g, jnp.maximum(p - 1, 0)])
                    high = jnp.where(
                        p == BINS - 1, FBAND, cut_ref[j + g, jnp.minimum(p, BINS - 2)])

                    @pl.when(high - low > NARROW)
                    def _():
                        column = lax.broadcasted_iota(jnp.int32, (1, 2 * FBAND), 1) % FBAND
                        mask = jnp.where((column >= low) & (column < high), 1.0, 0.0)
                        masked = prod[own, :] * mask.astype(jnp.bfloat16)
                        z = jnp.dot(masked, inverse_ref[...], preferred_element_type=jnp.float32)
                        z = z * z
                        squares[own, :] += BINS * (z[:, :STRIDE] + z[:, STRIDE:])

                    return carry

                lax.fori_loop(0, BINS, one_bin, 0)

    def consume(j, squares, mag):
        for g in range(GROUP):
            network = None
            for d in range(DET):
                own = slice(g * rows + d * blocks, g * rows + (d + 1) * blocks)
                scale = sig_ref[j + g][d:d + 1, :1]
                strength = mag[own, :] * scale
                reduced = (squares[own, :] - mag[own, :]) * (scale * (1.0 / (2.0 * BINS - 2.0)))
                reduced = jnp.maximum(reduced, 1.0)
                cube = reduced * reduced * reduced + 1.0
                weighted = strength * jnp.exp2(jnp.log(cube) * (-1.0 / (3.0 * math.log(2.0))))
                best[d] = jnp.maximum(best[d], strength)
                best[DET + d] = jnp.maximum(best[DET + d], weighted)
                network = weighted if network is None else network + weighted
            best[2 * DET] = jnp.maximum(best[2 * DET], network)

    def step(i, now, later):
        consume(i * GROUP, *now)
        widest = produce((i + 1) * GROUP, *later)
        add_wide((i + 1) * GROUP, widest, later[0])

    slot_a, slot_b = (squares_a, mag_a), (squares_b, mag_b)
    add_wide(0, produce(0, *slot_a), squares_a)

    def pair(i, carry):
        step(2 * i, slot_a, slot_b)
        step(2 * i + 1, slot_b, slot_a)
        return carry

    groups = count // GROUP
    lax.fori_loop(0, (groups - 1) // 2, pair, 0)
    if groups % 2 == 0:
        step(groups - 2, slot_a, slot_b)
        consume(count - GROUP, *slot_b)
    else:
        consume(count - GROUP, *slot_a)
    for d in range(2 * DET + 1):
        gain = 1.0 if d < DET else 2.0 ** (1.0 / 6.0)
        root = jnp.sqrt(best[d]) * gain
        for c in range(STRIDE // 128):
            turned[c, pl.ds(d, blocks, stride=8), :] = root[:, c * 128:(c + 1) * 128]
    for b in range(blocks):
        for c in range(STRIDE // 128):
            at = b * STRIDE + c * 128
            out_ref[:, at:at + 128] = turned[c, 8 * b:8 * b + 2 * DET + 1, :]


def scoring_call(count, blocks):
    f32 = jnp.float32
    rows = DET * blocks
    vmem = pl.BlockSpec(memory_space=pltpu.VMEM)

    def scoring(*refs):
        score(count, blocks, *refs)

    return pl.pallas_call(
        scoring,
        out_shape=jax.ShapeDtypeStruct((2 * DET + 1, blocks * STRIDE), f32),
        in_specs=[pl.BlockSpec(memory_space=pltpu.SMEM)] + [vmem] * 6,
        out_specs=vmem,
        scratch_shapes=[
            pltpu.VMEM((GROUP * rows, 2 * FBAND), jnp.bfloat16),
            pltpu.VMEM((BINS * GROUP * rows, 2 * POINTS), jnp.bfloat16),
            pltpu.VMEM((2 * DET + 1, blocks, STRIDE), f32),
            pltpu.VMEM((GROUP * rows, STRIDE), f32), pltpu.VMEM((GROUP * rows, STRIDE), f32),
            pltpu.VMEM((GROUP * rows, STRIDE), f32), pltpu.VMEM((GROUP * rows, STRIDE), f32),
            pltpu.VMEM((STRIDE // 128, 8 * blocks, 128), f32),
        ],
        compiler_params=pltpu.CompilerParams(vmem_limit_bytes=40 * 2**20),
    )


def scoring_tables():
    inverse = rotation_table(FLOW + np.arange(FBAND), np.arange(STRIDE), BLOCK)
    sample = rotation_table(np.arange(POINTS), np.arange(POINTS), POINTS)
    spread = BINS * spread_table()
    return [jnp.asarray(table.astype(jnp.bfloat16)) for table in (inverse, sample, spread)]


def shards(strain, segment_valid, templates, durations, bin_edges):
    n_tm, n_tp = lax.axis_size("tm"), lax.axis_size("tmpl")
    me_tp = lax.axis_index("tmpl")
    span_len = strain.shape[1]
    piece = span_len // n_tp
    blocks = piece // STRIDE
    rows = DET * blocks
    per = templates.shape[0]
    count = per * n_tp
    pick = STRIDE // SEG

    start = me_tp * piece
    follow = lax.rem(me_tp + 1, n_tp) * piece
    own = lax.dynamic_slice_in_dim(strain, start, piece, 1).reshape(rows, STRIDE)
    next_block = lax.dynamic_slice_in_dim(strain, follow, STRIDE, 1)
    within = jnp.arange(TLEN, dtype=jnp.int32)[None, :] < durations[:, None]
    shaped = jnp.where(within, templates, 0.0)
    spare = EXTRA - 2 * DET - per
    x = jnp.concatenate(
        [own, next_block, strain[:, :STRIDE], shaped, jnp.zeros((spare, STRIDE), jnp.float32)])
    own_valid = lax.dynamic_slice_in_dim(segment_valid, start // SEG, pick * blocks, 1)
    next_valid = lax.dynamic_slice_in_dim(segment_valid, follow // SEG, pick, 1)
    valid = jnp.concatenate(
        [own_valid.reshape(rows, pick), next_valid, segment_valid[:, :pick],
         jnp.ones((per + spare, pick), jnp.int32)]).astype(jnp.float32)
    edges = jnp.pad(bin_edges.astype(jnp.float32), ((0, 0), (0, 128 - bin_edges.shape[1])))

    vmem = pl.BlockSpec(memory_space=pltpu.VMEM)
    dma = pltpu.SemaphoreType.DMA
    f32 = jnp.float32

    def body(*refs):
        prepare(n_tm, n_tp, blocks, *refs)

    spec, filt, sig, cut = pl.pallas_call(
        body,
        out_shape=(
            jax.ShapeDtypeStruct((rows, 2 * FBAND), f32),
            jax.ShapeDtypeStruct((count, DET, 2 * FBAND), f32),
            jax.ShapeDtypeStruct((count, DET, 128), f32),
            jax.ShapeDtypeStruct((n_tp, per, 128), jnp.int32),
        ),
        in_specs=[vmem] * 4,
        out_specs=(vmem,) * 4,
        scratch_shapes=[
            pltpu.VMEM((DET, blocks + 8, 2 * FBAND), f32),
            pltpu.VMEM((DET, 2 * FBAND), f32),
            pltpu.VMEM((DET, 2 * FBAND), f32),
            pltpu.VMEM((n_tp, per, 2 * FBAND + 128), f32),
            pltpu.VMEM((n_tp, DET, FBAND), f32),
            pltpu.VMEM((n_tm, DET, FBAND), f32),
            dma((2,)), dma((n_tp,)), dma((n_tp,)), dma((n_tp,)), dma((n_tp,)),
            dma((n_tm,)), dma((n_tm,)),
        ],
        compiler_params=pltpu.CompilerParams(
            collective_id=0, has_side_effects=True, vmem_limit_bytes=40 * 2**20),
    )(x, valid, edges, jnp.asarray(split_table(forward_table())))

    return scoring_call(count, blocks)(
        cut.reshape(count, 128)[:, :BINS], spec, filt, sig, *scoring_tables())


def solution(mesh):
    placed = (P(None, "tm"), P(None, "tm"), P("tmpl", None), P("tmpl"), P("tmpl", None))
    return jax.shard_map(
        shards, mesh=mesh, in_specs=placed, out_specs=P(None, ("tm", "tmpl")), check_vma=False
    )
```
